256 devices in a mesh: dp: 32 (over y, x, core), tensor: 8 (over z).
Axes of the slice: x: 4, y: 4, z: 8, core: 2. Of those that a mesh axis runs over, the one named last changes fastest.
Arguments:
- inputs: bfloat16 [16384, 2560], P('dp'), may hold values from -6 to 6
- cotangent: bfloat16 [16384, 13312], P('dp', 'tensor'), may hold values from -48 to 48
- seed_values: int32 [13312, 32], P('tensor'), may hold values from -64 to 64
- counts: int32 [32], P('dp'), may hold values from 1 to 512, 8192 in all
Outputs:
- new_error: bfloat16 [32, 2560, 13312], P('dp', None, 'tensor')
- q_factor: float32 [13312, 32], P('tensor')
The draws below stay inside these ranges and needn't reach their ends.
Inputs may be any that keep to these rules, and one draw needn't show every extreme that they name: `counts`: each replica has at least one live token; some replica fills all 512 slots.
All inputs are finite; a program needn't handle non-finite values. No bound on the sum of `counts` on one device may be relied on, other than what follows from the above.
Results may differ from the reference program's by a relative error of at most 0.001.
Values sent between devices are 32-bit elements; how exact they have to be, the bound alone decides.
A program may use at most 128 MiB of HBM per device.

```python
import math
import jax
import jax.numpy as jnp
import numpy as np
from jax import lax

D = 2560
FF = 13312
RANK = 32
TOK_CAP = 512
REPLICAS = 32
TOKENS = 16384
N_DP = 32


def with_ends(drawn, own_key, least, largest):
    longest = drawn.shape.index(max(drawn.shape))
    spots = []
    for shift in (0, 1):
        where = [jax.random.randint(jax.random.fold_in(own_key, axis), (), 0, length) for axis, length in enumerate(drawn.shape)]
        where[longest] = (where[longest] + shift) % drawn.shape[longest]
        spots.append(tuple(where))
    return drawn.at[spots[0]].set(least).at[spots[1]].set(largest)


def shard_levels(key, dims, cuts, least, high):
    loudness = 1.0
    for dim, blocks in cuts:
        draws = jax.random.uniform(jax.random.fold_in(jax.random.fold_in(key, 6), dim), (blocks,), jnp.float32, least / len(cuts), high / len(cuts))
        loudness = loudness * jnp.repeat(jnp.exp(draws), dims[dim] // blocks).reshape((-1,) + (1,) * (len(dims) - 1 - dim))
    return loudness


def split_up(number_of, total, reach, skew):
    portions = [(1 << 20) // math.isqrt(standing ** skew) + 1 for standing in range(2, number_of + 1)]
    surplus, holding = total - reach - (number_of - 1), [1] * (number_of - 1)
    while surplus > 0:
        free = [i for i in range(number_of - 1) if holding[i] < reach]
        pool, budget = sum([portions[i] for i in free]), surplus
        for i in free:
            more = min(reach - holding[i], max(1, budget * portions[i] // pool), surplus)
            holding[i] = holding[i] + more
            surplus = surplus - more
    return np.array([reach] + holding)


def ragged(own_key, count, total, most, skew):
    if count == 2:
        one = jax.random.randint(own_key, (), max(1, total - most), min(most, total - 1) + 1)
        return jnp.stack([one, total - one])
    lengths = jnp.asarray(split_up(count, total, most, skew), jnp.int32)
    couples = (count - 1) // 2
    donor, receiver = lengths[1:1 + 2 * couples:2], lengths[2:2 + 2 * couples:2]
    room = jnp.minimum(donor - 1, most - receiver)
    shifted = jax.random.randint(jax.random.fold_in(own_key, 1), (couples,), 0, 1 << 20) % (room + 1)
    lengths = lengths.at[1:1 + 2 * couples:2].set(donor - shifted).at[2:2 + 2 * couples:2].set(receiver + shifted)
    return lengths[jax.random.permutation(jax.random.fold_in(own_key, 2), count)]


def normal_values(own_key, shape, width, bound, shards=(), kind=jnp.bfloat16):
    drawn = width * jax.random.normal(own_key, shape, jnp.float32)
    if shards:
        drawn = drawn * shard_levels(own_key, shape, shards, -0.22, 0.18)
    return jnp.clip(drawn, -bound, bound).astype(kind)


def setup_inputs(seed: int = 0) -> dict:
    streams_of = jax.random.split(jax.random.key(seed), 5)
    return {
        "inputs": normal_values(streams_of[0], (TOKENS, D), 1.0, 6.0, ((0, 32),)),
        "cotangent": normal_values(streams_of[1], (TOKENS, FF), 8.0, 48.0, ((0, 32), (1, 8))),
        "seed_values": with_ends(jax.random.randint(streams_of[2], (FF, RANK), -64, 65), jax.random.fold_in(streams_of[2], 1), -64, 64).astype(jnp.int32),
        "counts": ragged(streams_of[3], REPLICAS, TOK_CAP // 2 * REPLICAS, TOK_CAP, 2).astype(jnp.int32),
    }


def orthonormal(matrix):
    cols = matrix.shape[1]
    places = jnp.arange(cols)

    def orth_step(column_index, current):
        column = lax.dynamic_slice_in_dim(current, column_index, 1, 1)
        earlier = (places < column_index).astype(jnp.float32)[:, None]
        for repeat in range(2):
            coeffs = jnp.dot(current.T, column, precision=lax.Precision.HIGHEST) * earlier
            column = column - jnp.dot(current, coeffs, precision=lax.Precision.HIGHEST)
        column = column / jnp.sqrt(jnp.sum(column * column))
        return lax.dynamic_update_slice_in_dim(current, column, column_index, 1)
    return lax.fori_loop(0, cols, orth_step, matrix)

def reference(inputs, cotangent, seed_values, counts):
    slot_place = jnp.arange(TOK_CAP, dtype=jnp.int32)[None, :] < counts[:, None]
    live_rows = slot_place.reshape(TOKENS, 1)
    live_inputs = jnp.where(live_rows, inputs, jnp.zeros_like(inputs))
    token_count = jnp.sum(counts).astype(jnp.float32)
    grad_scale = N_DP / token_count
    start_factor = seed_values.astype(jnp.float32) / 64.0
    wide_inputs = live_inputs.astype(jnp.float32)
    wide_cotangent = cotangent.astype(jnp.float32)
    narrow = jnp.dot(wide_cotangent, start_factor, precision=lax.Precision.HIGHEST)
    p_matrix = jnp.dot(wide_inputs.T, narrow, precision=lax.Precision.HIGHEST) / token_count
    ortho_basis = orthonormal(p_matrix)
    projected = jnp.dot(wide_inputs, ortho_basis, precision=lax.Precision.HIGHEST)
    q_factor = jnp.dot(wide_cotangent.T, projected, precision=lax.Precision.HIGHEST) / token_count
    approx = jnp.dot(ortho_basis, q_factor.T, precision=lax.Precision.HIGHEST)
    input_blocks = live_inputs.reshape(N_DP, TOK_CAP, D)
    cotangent_blocks = cotangent.reshape(N_DP, TOK_CAP, FF)

    def replica_error(pair):
        weight_grad = jnp.dot(pair[0].T, pair[1], preferred_element_type=jnp.float32)
        return (weight_grad * grad_scale - approx).astype(jnp.bfloat16)
    new_error = lax.map(replica_error, (input_blocks, cotangent_blocks))
    return (new_error, q_factor)
```

```python
import functools

import jax
import jax.numpy as jnp
from jax import lax
from jax.experimental import pallas as pl
from jax.experimental.pallas import tpu as pltpu
from jax.sharding import PartitionSpec as P

F32, BF16 = jnp.float32, jnp.bfloat16
LANES = 128
NT = (((1,), (1,)), ((), ()))
TN = (((0,), (0,)), ((), ()))


def round_up(value, unit):
    return -(-value // unit) * unit


def split3(value):
    high = value.astype(BF16)
    rest = value - high.astype(F32)
    mid = rest.astype(BF16)
    low = (rest - mid.astype(F32)).astype(BF16)
    return high, mid, low


def fold3(stacked):
    rows = stacked.shape[0] // 3
    return stacked[:rows] + stacked[rows : 2 * rows] + stacked[2 * rows :]


def exact_dot(left, right, dims=(((1,), (0,)), ((), ()))):
    return lax.dot_general(left, right, dims, precision=lax.Precision.HIGHEST, preferred_element_type=F32)


def inverse_cholesky(gram):
    size = gram.shape[0]
    row = lax.broadcasted_iota(jnp.int32, (size, size), 0)
    col = lax.broadcasted_iota(jnp.int32, (size, size), 1)
    left, right = gram, (row == col).astype(F32)
    below = lax.broadcasted_iota(jnp.int32, (size, 1), 0)
    for k in range(size - 1):
        pivot = left[k : k + 1, k : k + 1]
        factor = jnp.where(below > k, left[:, k : k + 1] / pivot, 0.0)
        left, right = left - factor * left[k : k + 1, :], right - factor * right[k : k + 1, :]
    diagonal = jnp.sum(jnp.where(row == col, left, 0.0), axis=1, keepdims=True)
    guess = lax.rsqrt(diagonal)
    guess = guess * (1.5 - 0.5 * diagonal * guess * guess)
    return right * guess


def spread(ref, value, pitch):
    rows, width = value.shape
    for j in range(width // LANES):
        ref[pl.ds(j, rows, stride=pitch), :] = value[:, j * LANES : (j + 1) * LANES]


def collect(ref, rows, width, pitch):
    return jnp.concatenate([ref[pl.ds(j, rows, stride=pitch), :] for j in range(width // LANES)], axis=1)


def add_blocks(ref, blocks, pitch):
    total = ref[0:pitch, :]
    for i in range(1, blocks):
        total = total + ref[i * pitch : (i + 1) * pitch, :]
    return total


def exchange_kernel(
    n, nz, pitch_p, pitch_w,
    count_ref, x_hbm, c_hbm, s_hbm,
    basis_ref, qcat_ref, qt_ref, scale_ref,
    x, c, s, snd1, rcv1, zsnd, zrcv, pfull, snd2, rcv2, wfull,
    load_sem, send_sem, recv_sem,
):
    me, mz = lax.axis_index("dp"), lax.axis_index("tensor")
    tokens, d = x.shape
    f = c.shape[1]

    loads = [pltpu.make_async_copy(src, dst, load_sem.at[i]) for i, (src, dst) in enumerate(((c_hbm, c), (s_hbm, s), (x_hbm, x)))]
    for load in loads:
        load.start()

    barrier = pltpu.get_barrier_semaphore()

    @pl.loop(1, n)
    def _(k):
        pl.semaphore_signal(barrier, inc=1, device_id={"dp": lax.rem(me + k, n)}, device_id_type=pl.DeviceIdType.MESH)

    @pl.loop(1, nz)
    def _(k):
        pl.semaphore_signal(barrier, inc=1, device_id={"tensor": lax.rem(mz + k, nz)}, device_id_type=pl.DeviceIdType.MESH)

    def block(ref, index, pitch):
        return ref.at[pl.ds(pl.multiple_of(index * pitch, 8), pitch), :]

    def send(phase, axis, size, place, source, target):
        @pl.loop(1, size)
        def _(k):
            peer = lax.rem(place + k, size)
            pltpu.make_async_remote_copy(
                src_ref=source(peer), dst_ref=target, send_sem=send_sem.at[phase], recv_sem=recv_sem.at[phase],
                device_id={axis: peer}, device_id_type=pl.DeviceIdType.MESH,
            ).start()

    def wait(sem, ref, rows):
        part = ref.at[pl.ds(0, rows), :]
        pltpu.make_async_copy(part, part, sem).wait()

    live = lax.broadcasted_iota(jnp.int32, (n, tokens), 1) < count_ref[0]

    loads[0].wait()
    loads[1].wait()
    narrow = lax.dot_general(s[...].astype(F32).astype(BF16), c[...], NT, preferred_element_type=F32)
    narrow = jnp.concatenate(split3(jnp.where(live, narrow, 0.0)), axis=0)
    loads[2].wait()
    spread(snd1, fold3(jnp.dot(narrow, x[...], preferred_element_type=F32)), pitch_p)
    counted = jnp.full((n, LANES), count_ref[0], jnp.int32).astype(F32)
    snd1[pl.ds(d // LANES, n, stride=pitch_p), :] = counted
    for j in range(d // LANES + 1, pitch_p):
        snd1[pl.ds(j, n, stride=pitch_p), :] = jnp.zeros((n, LANES), F32)
    rcv1[pl.ds(pl.multiple_of(me * pitch_p, 8), pitch_p), :] = snd1[pl.ds(pl.multiple_of(me * pitch_p, 8), pitch_p), :]

    pl.semaphore_wait(barrier, n - 1 + nz - 1)
    send(0, "dp", n, me, lambda peer: block(snd1, peer, pitch_p), block(rcv1, me, pitch_p))
    wait(recv_sem.at[0], rcv1, (n - 1) * pitch_p)

    total = add_blocks(rcv1, n, pitch_p)
    token_count = total[d // LANES : d // LANES + 1, :]
    mine = total / (64.0 * token_count)
    zsnd[...] = mine
    zrcv[pl.ds(pl.multiple_of(mz * pitch_p, 8), pitch_p), :] = mine
    send(1, "tensor", nz, mz, lambda peer: zsnd, block(zrcv, mz, pitch_p))
    wait(recv_sem.at[1], zrcv, (nz - 1) * pitch_p)

    pfull[pl.ds(pl.multiple_of(me * pitch_p, 8), pitch_p), :] = add_blocks(zrcv, nz, pitch_p)
    send(2, "dp", n, me, lambda peer: block(pfull, me, pitch_p), block(pfull, me, pitch_p))
    wait(recv_sem.at[2], pfull, (n - 1) * pitch_p)

    left = collect(pfull, n, d, pitch_p)
    projected = fold3(lax.dot_general(jnp.concatenate(split3(left), axis=0), x[...], NT, preferred_element_type=F32))
    projected = jnp.concatenate(split3(jnp.where(live, projected, 0.0)), axis=0)
    spread(snd2, fold3(jnp.dot(projected, c[...], preferred_element_type=F32)), pitch_w)
    for j in range(f // LANES, pitch_w):
        snd2[pl.ds(j, n, stride=pitch_w), :] = jnp.zeros((n, LANES), F32)
    rcv2[pl.ds(pl.multiple_of(me * pitch_w, 8), pitch_w), :] = snd2[pl.ds(pl.multiple_of(me * pitch_w, 8), pitch_w), :]
    send(3, "dp", n, me, lambda peer: block(snd2, peer, pitch_w), block(rcv2, me, pitch_w))

    first = inverse_cholesky(exact_dot(left, left, NT))
    nearly = exact_dot(first, left)

    wait(recv_sem.at[3], rcv2, (n - 1) * pitch_w)
    wfull[pl.ds(pl.multiple_of(me * pitch_w, 8), pitch_w), :] = add_blocks(rcv2, n, pitch_w) / token_count
    send(4, "dp", n, me, lambda peer: block(wfull, me, pitch_w), block(wfull, me, pitch_w))

    second = inverse_cholesky(exact_dot(nearly, nearly, NT))
    basis = exact_dot(second, nearly)
    whole = exact_dot(second, first)
    h, m, l = split3(basis)
    basis_ref[...] = jnp.concatenate((h, h, m, h, l, m), axis=0)
    scale_ref[...] = jnp.broadcast_to(float(n) / token_count, scale_ref.shape)

    wait(recv_sem.at[4], wfull, (n - 1) * pitch_w)
    q = exact_dot(whole, collect(wfull, n, f, pitch_w))
    qt_ref[...] = q
    h, m, l = split3(q)
    qcat_ref[...] = jnp.concatenate((h, m, h, l, h, m), axis=0)

    wait(send_sem.at[0], snd1, (n - 1) * pitch_p)
    wait(send_sem.at[1], zrcv, (nz - 1) * pitch_p)
    wait(send_sem.at[2], pfull, (n - 1) * pitch_p)
    wait(send_sem.at[3], snd2, (n - 1) * pitch_w)
    wait(send_sem.at[4], wfull, (n - 1) * pitch_w)


def error_kernel(count_ref, x_ref, c_ref, basis_ref, qcat_ref, scale_ref, qt_in, out_ref, qt_out, live_c):
    @pl.when(pl.program_id(0) == 0)
    def _():
        position = lax.broadcasted_iota(jnp.int32, live_c.shape, 0)
        live_c[...] = jnp.where(position < count_ref[0], c_ref[...], jnp.zeros_like(c_ref))
        qt_out[...] = qt_in[...]

    grad = lax.dot_general(x_ref[...], live_c[...], TN, preferred_element_type=F32)
    approx = lax.dot_general(basis_ref[...], qcat_ref[...], TN, preferred_element_type=F32)
    out_ref[...] = (grad * scale_ref[0:1, 0:1] - approx).astype(BF16)


def shards(inputs, cotangent, seed_values, counts):
    n, nz = lax.axis_size("dp"), lax.axis_size("tensor")
    tokens, d = inputs.shape
    f = cotangent.shape[1]
    rank = seed_values.shape[1]
    pitch_p, pitch_w = round_up(d // LANES + 1, 8), round_up(f // LANES, 8)
    smem, anywhere = pl.BlockSpec(memory_space=pltpu.SMEM), pl.BlockSpec(memory_space=pl.ANY)
    vmem = pl.BlockSpec(memory_space=pltpu.VMEM)
    basis, qcat, qt, scale = pl.pallas_call(
        functools.partial(exchange_kernel, n, nz, pitch_p, pitch_w),
        out_shape=(
            jax.ShapeDtypeStruct((6 * rank, d), BF16),
            jax.ShapeDtypeStruct((6 * rank, f), BF16),
            jax.ShapeDtypeStruct((rank, f), F32),
            jax.ShapeDtypeStruct((8, LANES), F32),
        ),
        in_specs=[smem, anywhere, anywhere, anywhere],
        out_specs=(vmem,) * 4,
        scratch_shapes=[
            pltpu.VMEM((tokens, d), BF16),
            pltpu.VMEM((tokens, f), BF16),
            pltpu.VMEM((rank, f), jnp.int32),
            pltpu.VMEM((n * pitch_p, LANES), F32),
            pltpu.VMEM((n * pitch_p, LANES), F32),
            pltpu.VMEM((pitch_p, LANES), F32),
            pltpu.VMEM((nz * pitch_p, LANES), F32),
            pltpu.VMEM((n * pitch_p, LANES), F32),
            pltpu.VMEM((n * pitch_w, LANES), F32),
            pltpu.VMEM((n * pitch_w, LANES), F32),
            pltpu.VMEM((n * pitch_w, LANES), F32),
            pltpu.SemaphoreType.DMA((3,)),
            pltpu.SemaphoreType.DMA((5,)),
            pltpu.SemaphoreType.DMA((5,)),
        ],
        compiler_params=pltpu.CompilerParams(collective_id=0, has_side_effects=True, vmem_limit_bytes=32 << 20),
        name="exchange",
    )(counts, inputs, cotangent, seed_values.T)

    rows = 256 if d % 256 == 0 else LANES
    new_error, qt = pl.pallas_call(
        error_kernel,
        grid=(d // rows,),
        out_shape=(jax.ShapeDtypeStruct((d, f), BF16), jax.ShapeDtypeStruct((rank, f), F32)),
        in_specs=[
            smem,
            pl.BlockSpec((tokens, rows), lambda i: (0, i)),
            pl.BlockSpec((tokens, f), lambda i: (0, 0)),
            pl.BlockSpec((6 * rank, rows), lambda i: (0, i)),
            pl.BlockSpec((6 * rank, f), lambda i: (0, 0)),
            pl.BlockSpec((8, LANES), lambda i: (0, 0)),
            pl.BlockSpec((rank, f), lambda i: (0, 0)),
        ],
        out_specs=(pl.BlockSpec((rows, f), lambda i: (i, 0)), pl.BlockSpec((rank, f), lambda i: (0, 0))),
        scratch_shapes=[pltpu.VMEM((tokens, f), BF16)],
        compiler_params=pltpu.CompilerParams(vmem_limit_bytes=32 << 20),
        name="error",
    )(counts, inputs, cotangent, basis, qcat, scale, qt)
    return (new_error[None], qt.T)


def solution(mesh):
    return jax.shard_map(
        shards,
        mesh=mesh,
        in_specs=(P("dp", None), P("dp", "tensor"), P("tensor", None), P("dp")),
        out_specs=(P("dp", None, "tensor"), P("tensor", None)),
        check_vma=False,
    )
```

```python
import functools
import math

import jax
import jax.numpy as jnp
from jax import lax
from jax.experimental import pallas as pl
from jax.experimental.pallas import tpu as pltpu
from jax.sharding import PartitionSpec as P

F32, BF16 = jnp.float32, jnp.bfloat16
LANES = 128
NT = (((1,), (1,)), ((), ()))
TN = (((0,), (0,)), ((), ()))


def round_up(value, unit):
    return -(-value // unit) * unit


def split3(value):
    high = value.astype(BF16)
    rest = value - high.astype(F32)
    mid = rest.astype(BF16)
    low = (rest - mid.astype(F32)).astype(BF16)
    return high, mid, low


def fold3(stacked):
    rows = stacked.shape[0] // 3
    return stacked[:rows] + stacked[rows : 2 * rows] + stacked[2 * rows :]


def exact_dot(left, right, dims=(((1,), (0,)), ((), ()))):
    return lax.dot_general(left, right, dims, precision=lax.Precision.HIGHEST, preferred_element_type=F32)


def inverse_cholesky(gram, group=8):
    size = gram.shape[0]
    row = lax.broadcasted_iota(jnp.int32, (size, size), 0)
    col = lax.broadcasted_iota(jnp.int32, (size, size), 1)
    below = lax.broadcasted_iota(jnp.int32, (size, 1), 0)
    diagonal = jnp.sum(jnp.where(row == col, gram, 0.0), axis=1, keepdims=True)
    floors = jnp.broadcast_to(1e-6 * diagonal, (size, size))
    left, right, scale = gram, (row == col).astype(F32), jnp.ones((size, size), F32)
    for start in range(0, size, group):
        columns = [jnp.broadcast_to(left[:, start + j : start + j + 1], (size, size)) for j in range(group)]
        for j in range(group):
            k = start + j
            pivot = jnp.maximum(columns[j][k : k + 1, :], floors[k : k + 1, :])
            factor = jnp.where(below > k, columns[j] / pivot, 0.0)
            scale = jnp.where(below == k, pivot, scale)
            for i in range(j + 1, group):
                columns[i] = columns[i] - factor * columns[i][k : k + 1, :]
            left, right = left - factor * left[k : k + 1, :], right - factor * right[k : k + 1, :]
    guess = lax.rsqrt(scale)
    return right * (guess * (1.5 - 0.5 * scale * guess * guess))


def spread(ref, value, pitch):
    rows, width = value.shape
    for j in range(width // LANES):
        ref[pl.ds(j, rows, stride=pitch), :] = value[:, j * LANES : (j + 1) * LANES]


def collect(ref, rows, width, pitch):
    return jnp.concatenate([ref[pl.ds(j, rows, stride=pitch), :] for j in range(width // LANES)], axis=1)


def add_blocks(ref, blocks, pitch, rows):
    total = ref[0:rows, :]
    for i in range(1, blocks):
        total = total + ref[i * pitch : i * pitch + rows, :]
    return total


def ring_distance(step, size):
    return min(step, size - step)


def plane_peers(me, n):
    side = math.isqrt(n // 2)
    y, x, core = me // (2 * side), me // 2 % side, me % 2
    steps = [(dy, dx, dc) for dy in range(side) for dx in range(side) for dc in range(2) if dy or dx or dc]
    steps.sort(key=lambda step: -ring_distance(step[0], side) - ring_distance(step[1], side))
    return [((y + dy) % side * side + (x + dx) % side) * 2 + (core + dc) % 2 for dy, dx, dc in steps]


def line_peers(me, n):
    return [(me + step) % n for step in sorted(range(1, n), key=lambda step: -ring_distance(step, n))]


def exchange_kernel(
    n, nz, rows_p, rows_w, pitch_p, pitch_w, tile,
    count_ref, x_hbm, c_hbm, s_hbm,
    grad_ref, basis_ref, qcat_ref, qt_ref, scale_ref,
    x, c, s, live_c, snd1, rcv1, zsnd, zrcv, pfull, snd2, rcv2, wfull, nearly, whole,
    load_sem, send_sem, recv_sem,
):
    me, mz = lax.axis_index("dp"), lax.axis_index("tensor")
    tokens, d = x.shape
    f = c.shape[1]
    in_plane, in_line = plane_peers(me, n), line_peers(mz, nz)

    loads = [pltpu.make_async_copy(src, dst, load_sem.at[i]) for i, (src, dst) in enumerate(((c_hbm, c), (s_hbm, s), (x_hbm, x)))]
    for load in loads:
        load.start()

    barrier = pltpu.get_barrier_semaphore()
    for axis, peers in (("tensor", in_line), ("dp", in_plane)):
        for peer in peers:
            pl.semaphore_signal(barrier, inc=1, device_id={axis: peer}, device_id_type=pl.DeviceIdType.MESH)

    def block(ref, index, pitch, rows):
        return ref.at[pl.ds(pl.multiple_of(index * pitch, 8), rows), :]

    def send(phase, axis, peers, source, target):
        for peer in peers:
            pltpu.make_async_remote_copy(
                src_ref=source(peer), dst_ref=target, send_sem=send_sem.at[phase], recv_sem=recv_sem.at[phase],
                device_id={axis: peer}, device_id_type=pl.DeviceIdType.MESH,
            ).start()

    def wait(sem, ref, rows):
        part = ref.at[pl.ds(0, rows), :]
        pltpu.make_async_copy(part, part, sem).wait()

    def weight_grad(first, last):
        @pl.loop(first, last)
        def _(i):
            here = pl.ds(pl.multiple_of(i * tile, tile), tile)
            grad_ref[here, :] = lax.dot_general(x[:, here], live_c[...], TN, preferred_element_type=F32)

    live = lax.broadcasted_iota(jnp.int32, (n, tokens), 1) < count_ref[0]
    own_p, own_w = pl.ds(pl.multiple_of(me * pitch_p, 8), rows_p), pl.ds(pl.multiple_of(me * pitch_w, 8), rows_w)
    tiles = d // tile

    loads[0].wait()
    loads[1].wait()
    narrow = lax.dot_general((s[...].astype(F32) / 64.0).astype(BF16), c[...], NT, preferred_element_type=F32)
    narrow = jnp.concatenate(split3(jnp.where(live, narrow, 0.0)), axis=0)
    loads[2].wait()
    spread(snd1, fold3(jnp.dot(narrow, x[...], preferred_element_type=F32)), pitch_p)
    rcv1[own_p, :] = snd1[own_p, :]

    pl.semaphore_wait(barrier, n - 1 + nz - 1)
    send(0, "dp", in_plane, lambda peer: block(snd1, peer, pitch_p, rows_p), block(rcv1, me, pitch_p, rows_p))
    position = lax.broadcasted_iota(jnp.int32, live_c.shape, 0)
    live_c[...] = jnp.where(position < count_ref[0], c[...], jnp.zeros_like(c))
    weight_grad(0, tiles // 2)
    wait(recv_sem.at[0], rcv1, (n - 1) * rows_p)

    mine = add_blocks(rcv1, n, pitch_p, rows_p)
    zsnd[...] = mine
    zrcv[pl.ds(pl.multiple_of(mz * pitch_p, 8), rows_p), :] = mine
    send(1, "tensor", in_line, lambda peer: zsnd, block(zrcv, mz, pitch_p, rows_p))
    weight_grad(tiles // 2, tiles)
    wait(recv_sem.at[1], zrcv, (nz - 1) * rows_p)

    pfull[own_p, :] = add_blocks(zrcv, nz, pitch_p, rows_p)
    send(2, "dp", in_plane, lambda peer: block(pfull, me, pitch_p, rows_p), block(pfull, me, pitch_p, rows_p))
    wait(recv_sem.at[2], pfull, (n - 1) * rows_p)

    left = collect(pfull, n, d, pitch_p)
    projected = fold3(lax.dot_general(jnp.concatenate(split3(left), axis=0), x[...], NT, preferred_element_type=F32))
    projected = jnp.concatenate(split3(jnp.where(live, projected, 0.0)), axis=0)
    spread(snd2, fold3(jnp.dot(projected, c[...], preferred_element_type=F32)), pitch_w)
    snd2[pl.ds(rows_w, n, stride=pitch_w), :] = jnp.full((n, LANES), count_ref[0], jnp.int32).astype(F32)
    counted = pl.ds(pl.multiple_of(me * pitch_w, 8), rows_w + 1)
    rcv2[counted, :] = snd2[counted, :]
    send(3, "dp", in_plane, lambda peer: block(snd2, peer, pitch_w, rows_w + 1), block(rcv2, me, pitch_w, rows_w + 1))

    nearly[...] = left

    def orthonormalize():
        step = inverse_cholesky(exact_dot(nearly[...], nearly[...], NT))
        nearly[...] = exact_dot(step, nearly[...])
        return step

    @pl.when(me >= 0)
    def _():
        once = orthonormalize()
        whole[...] = exact_dot(orthonormalize(), once)

    wait(recv_sem.at[3], rcv2, (n - 1) * (rows_w + 1))
    total = add_blocks(rcv2, n, pitch_w, rows_w + 1)
    token_count = total[rows_w : rows_w + 1, :]
    wfull[own_w, :] = total[0:rows_w, :] / token_count
    send(4, "dp", in_plane, lambda peer: block(wfull, me, pitch_w, rows_w), block(wfull, me, pitch_w, rows_w))

    @pl.when(me >= 0)
    def _():
        whole[...] = exact_dot(orthonormalize(), whole[...])
        h, m, l = split3(nearly[...])
        basis_ref[...] = jnp.concatenate((h, h, m, h, l, m), axis=0).T
        scale_ref[...] = jnp.broadcast_to(float(n) / token_count, scale_ref.shape)

    wait(recv_sem.at[4], wfull, (n - 1) * rows_w)
    q = exact_dot(whole[...], collect(wfull, n, f, pitch_w))
    qt_ref[...] = q
    h, m, l = split3(q)
    qcat_ref[...] = jnp.concatenate((h, m, h, l, h, m), axis=0)

    wait(send_sem.at[0], snd1, (n - 1) * rows_p)
    wait(send_sem.at[1], zrcv, (nz - 1) * rows_p)
    wait(send_sem.at[2], pfull, (n - 1) * rows_p)
    wait(send_sem.at[3], snd2, (n - 1) * (rows_w + 1))
    wait(send_sem.at[4], wfull, (n - 1) * rows_w)


def error_kernel(tile, grad_ref, basis_ref, qcat_ref, qt_in, scale_ref, out_hbm, qt_hbm, out, sem):
    qt_copy = pltpu.make_async_copy(qt_in, qt_hbm, sem.at[1])
    qt_copy.start()

    @pl.loop(0, out.shape[0] // tile)
    def _(i):
        here = pl.ds(pl.multiple_of(i * tile, tile), tile)
        approx = jnp.dot(basis_ref[here, :], qcat_ref[...], preferred_element_type=F32)
        out[here, :] = (grad_ref[here, :] * scale_ref[0:1, 0:1] - approx).astype(BF16)
        pltpu.make_async_copy(out.at[here, :], out_hbm.at[here, :], sem.at[0]).start()

    pltpu.make_async_copy(out, out_hbm, sem.at[0]).wait()
    qt_copy.wait()


def largest_tile(length, limit):
    return max(tile for tile in range(LANES, limit + 1, LANES) if length % tile == 0)


def shards(inputs, cotangent, seed_values, counts):
    n, nz = lax.axis_size("dp"), lax.axis_size("tensor")
    tokens, d = inputs.shape
    f = cotangent.shape[1]
    rank = seed_values.shape[1]
    rows_p, rows_w = d // LANES, f // LANES
    pitch_p, pitch_w = round_up(rows_p, 8), round_up(rows_w + 1, 8)
    smem, hbm, vmem = (pl.BlockSpec(memory_space=space) for space in (pltpu.SMEM, pltpu.HBM, pltpu.VMEM))
    held = [pltpu.with_memory_space_constraint(array, pltpu.HBM) for array in (inputs, cotangent, seed_values.T)]
    parts = pl.pallas_call(
        functools.partial(exchange_kernel, n, nz, rows_p, rows_w, pitch_p, pitch_w, largest_tile(d, 256)),
        out_shape=(
            pltpu.VMEM((d, f), F32),
            pltpu.VMEM((d, 6 * rank), BF16),
            pltpu.VMEM((6 * rank, f), BF16),
            pltpu.VMEM((rank, f), F32),
            pltpu.VMEM((8, LANES), F32),
        ),
        in_specs=[smem, hbm, hbm, hbm],
        out_specs=(vmem,) * 5,
        scratch_shapes=[
            pltpu.VMEM((tokens, d), BF16),
            pltpu.VMEM((tokens, f), BF16),
            pltpu.VMEM((rank, f), jnp.int32),
            pltpu.VMEM((tokens, f), BF16),
            pltpu.VMEM((n * pitch_p, LANES), F32),
            pltpu.VMEM((n * pitch_p, LANES), F32),
            pltpu.VMEM((rows_p, LANES), F32),
            pltpu.VMEM((nz * pitch_p, LANES), F32),
            pltpu.VMEM((n * pitch_p, LANES), F32),
            pltpu.VMEM((n * pitch_w, LANES), F32),
            pltpu.VMEM((n * pitch_w, LANES), F32),
            pltpu.VMEM((n * pitch_w, LANES), F32),
            pltpu.VMEM((rank, d), F32),
            pltpu.VMEM((rank, rank), F32),
            pltpu.SemaphoreType.DMA((3,)),
            pltpu.SemaphoreType.DMA((5,)),
            pltpu.SemaphoreType.DMA((5,)),
        ],
        compiler_params=pltpu.CompilerParams(collective_id=0, has_side_effects=True, vmem_limit_bytes=20 << 20),
        name="exchange",
    )(counts, *held)

    new_error, qt = pl.pallas_call(
        functools.partial(error_kernel, largest_tile(d, 640)),
        out_shape=(jax.ShapeDtypeStruct((d, f), BF16), jax.ShapeDtypeStruct((rank, f), F32)),
        in_specs=[vmem] * 5,
        out_specs=(hbm, hbm),
        scratch_shapes=[pltpu.VMEM((d, f), BF16), pltpu.SemaphoreType.DMA((2,))],
        compiler_params=pltpu.CompilerParams(vmem_limit_bytes=18 << 20),
        name="error",
    )(*parts)
    return (new_error[None], qt.T)


def solution(mesh):
    return jax.shard_map(
        shards,
        mesh=mesh,
        in_specs=(P("dp", None), P("dp", "tensor"), P("tensor", None), P("dp")),
        out_specs=(P("dp", None, "tensor"), P("tensor", None)),
        check_vma=False,
    )
```

```python
import functools
import math

import jax
import jax.numpy as jnp
from jax import lax
from jax.experimental import pallas as pl
from jax.experimental.pallas import tpu as pltpu
from jax.sharding import PartitionSpec as P

F32, BF16 = jnp.float32, jnp.bfloat16
LANES = 128
NT = (((1,), (1,)), ((), ()))
TN = (((0,), (0,)), ((), ()))


def round_up(value, unit):
    return -(-value // unit) * unit


def split3(value):
    high = value.astype(BF16)
    rest = value - high.astype(F32)
    mid = rest.astype(BF16)
    low = (rest - mid.astype(F32)).astype(BF16)
    return high, mid, low


def fold3(stacked):
    rows = stacked.shape[0] // 3
    return stacked[:rows] + stacked[rows : 2 * rows] + stacked[2 * rows :]


def exact_dot(left, right, dims=(((1,), (0,)), ((), ()))):
    return lax.dot_general(left, right, dims, precision=lax.Precision.HIGHEST, preferred_element_type=F32)


def inverse_cholesky(gram, group=8):
    size = gram.shape[0]
    row = lax.broadcasted_iota(jnp.int32, (size, size), 0)
    col = lax.broadcasted_iota(jnp.int32, (size, size), 1)
    below = lax.broadcasted_iota(jnp.int32, (size, 1), 0)
    diagonal = jnp.sum(jnp.where(row == col, gram, 0.0), axis=1, keepdims=True)
    floors = jnp.broadcast_to(1e-6 * diagonal, (size, size))
    left, right, scale = gram, (row == col).astype(F32), jnp.ones((size, size), F32)
    for start in range(0, size, group):
        columns = [jnp.broadcast_to(left[:, start + j : start + j + 1], (size, size)) for j in range(group)]
        for j in range(group):
            k = start + j
            pivot = jnp.maximum(columns[j][k : k + 1, :], floors[k : k + 1, :])
            factor = jnp.where(below > k, columns[j] / pivot, 0.0)
            scale = jnp.where(below == k, pivot, scale)
            for i in range(j + 1, group):
                columns[i] = columns[i] - factor * columns[i][k : k + 1, :]
            left, right = left - factor * left[k : k + 1, :], right - factor * right[k : k + 1, :]
    guess = lax.rsqrt(scale)
    return right * (guess * (1.5 - 0.5 * scale * guess * guess))


def spread(ref, value, pitch, first):
    rows, width = value.shape
    for j in range(width // LANES):
        ref[pl.ds(first + j, rows, stride=pitch), :] = value[:, j * LANES : (j + 1) * LANES]


def collect(ref, rows, pitch, part):
    return jnp.concatenate([ref[pl.ds(j, rows, stride=pitch), :] for j in range(*part)], axis=1)


def add_blocks(ref, blocks, pitch, part):
    total = ref[part[0] : part[1], :]
    for i in range(1, blocks):
        total = total + ref[i * pitch + part[0] : i * pitch + part[1], :]
    return total


def lanes(part):
    return pl.ds(part[0] * LANES, (part[1] - part[0]) * LANES)


def ring_distance(step, size):
    return min(step, size - step)


def plane_peers(me, n):
    side = math.isqrt(n // 2)
    y, x, core = me // (2 * side), me // 2 % side, me % 2
    steps = [(dy, dx, dc) for dy in range(side) for dx in range(side) for dc in range(2) if dy or dx or dc]
    far = [-ring_distance(step, side) for step in range(side)]
    steps.sort(key=lambda step: (far[step[0]] + far[step[1]], step[2], (3 * step[0] + 5 * step[1]) % side))
    return [((y + dy) % side * side + (x + dx) % side) * 2 + (core + dc) % 2 for dy, dx, dc in steps]


def line_peers(me, n):
    return [(me + step) % n for step in sorted(range(1, n), key=lambda step: -ring_distance(step, n))]


def exchange_kernel(
    n, nz, parts_p, parts_w, pitch_p, pitch_w, tile,
    count_ref, x_hbm, c_hbm, s_hbm,
    grad_ref, basis_ref, wcat_ref, w_ref, whole_ref, scale_ref,
    x, c, s, live_c, snd1a, snd1b, rcv1, zsnd, zrcv, pfulla, pfullb, snd2, rcv2, wfull, nearly, whole,
    load_sem, send_sem, recv_sem,
):
    me, mz = lax.axis_index("dp"), lax.axis_index("tensor")
    snd1, pfull = (snd1a, snd1b), (pfulla, pfullb)
    tokens, d = x.shape
    in_plane, in_line = plane_peers(me, n), line_peers(mz, nz)

    pairs = [(s_hbm, s), (c_hbm, c)] + [(x_hbm.at[:, lanes(part)], x.at[:, lanes(part)]) for part in parts_p]
    loads = [pltpu.make_async_copy(src, dst, load_sem.at[i]) for i, (src, dst) in enumerate(pairs)]
    for load in loads:
        load.start()

    barrier = pltpu.get_barrier_semaphore()
    for axis, peers in (("dp", in_plane), ("tensor", in_line)):
        for peer in peers:
            pl.semaphore_signal(barrier, inc=1, device_id={axis: peer}, device_id_type=pl.DeviceIdType.MESH)

    def rows_of(index, pitch, part):
        return pl.ds(index * pitch + part[0], part[1] - part[0])

    def send(phase, half, axis, peers, source, target):
        for peer in peers:
            pltpu.make_async_remote_copy(
                src_ref=source(peer), dst_ref=target, send_sem=send_sem.at[phase, half], recv_sem=recv_sem.at[phase, half],
                device_id={axis: peer}, device_id_type=pl.DeviceIdType.MESH,
            ).start()

    def wait(sem, ref, peers, part):
        here = ref.at[pl.ds(0, len(peers) * (part[1] - part[0])), :]
        pltpu.make_async_copy(here, here, sem).wait()

    def weight_grad(first, last):
        @pl.loop(first, last)
        def _(i):
            here = pl.ds(pl.multiple_of(i * tile, tile), tile)
            grad_ref[here, :] = lax.dot_general(x[:, here], live_c[...], TN, preferred_element_type=F32)

    live = lax.broadcasted_iota(jnp.int32, (n, tokens), 1) < count_ref[0]
    tiles = d // tile
    pitches_p = [round_up(part[1] - part[0], 8) for part in parts_p]
    counted_w = parts_w[:-1] + [(parts_w[-1][0], parts_w[-1][1] + 1)]

    loads[0].wait()
    loads[1].wait()
    narrow = lax.dot_general((s[...].astype(F32) / 64.0).astype(BF16), c[...], NT, preferred_element_type=F32)
    narrow = jnp.concatenate(split3(jnp.where(live, narrow, 0.0)), axis=0)
    for half, part in enumerate(parts_p):
        loads[2 + half].wait()
        spread(snd1[half], fold3(jnp.dot(narrow, x[:, lanes(part)], preferred_element_type=F32)), pitches_p[half], 0)
        rcv1[rows_of(me, pitch_p, part), :] = snd1[half][pl.ds(me * pitches_p[half], part[1] - part[0]), :]
        if half == 0:
            pl.semaphore_wait(barrier, n - 1 + nz - 1)
        send(0, half, "dp", in_plane, lambda peer: snd1[half].at[pl.ds(peer * pitches_p[half], part[1] - part[0]), :], rcv1.at[rows_of(me, pitch_p, part), :])
    position = lax.broadcasted_iota(jnp.int32, live_c.shape, 0)
    live_c[...] = jnp.where(position < count_ref[0], c[...], jnp.zeros_like(c))
    weight_grad(0, tiles // 2)

    for half, part in enumerate(parts_p):
        wait(recv_sem.at[0, half], rcv1, in_plane, part)
        mine = add_blocks(rcv1, n, pitch_p, part)
        zsnd[rows_of(0, pitch_p, part), :] = mine
        zrcv[rows_of(mz, pitch_p, part), :] = mine
        send(1, half, "tensor", in_line, lambda peer: zsnd.at[rows_of(0, pitch_p, part), :], zrcv.at[rows_of(mz, pitch_p, part), :])
    weight_grad(tiles // 2, tiles)

    for half, part in enumerate(parts_p):
        wait(recv_sem.at[1, half], zrcv, in_line, part)
        mine = pfull[half].at[pl.ds(me * pitches_p[half], part[1] - part[0]), :]
        mine[...] = add_blocks(zrcv, nz, pitch_p, part)
        send(2, half, "dp", in_plane, lambda peer: mine, mine)

    projected = 0.0
    for half, part in enumerate(parts_p):
        wait(recv_sem.at[2, half], pfull[half], in_plane, part)
        left = collect(pfull[half], n, pitches_p[half], (0, part[1] - part[0]))
        nearly[:, lanes(part)] = left
        projected = projected + lax.dot_general(
            jnp.concatenate(split3(left), axis=0), x[:, lanes(part)], NT, preferred_element_type=F32
        )
    projected = jnp.concatenate(split3(jnp.where(live, fold3(projected), 0.0)), axis=0)
    snd2[pl.ds(parts_w[-1][1], n, stride=pitch_w), :] = jnp.full((n, LANES), count_ref[0], jnp.int32).astype(F32)
    spread(snd2, fold3(jnp.dot(projected, c[...], preferred_element_type=F32)), pitch_w, 0)
    for half, part in enumerate(counted_w):
        rcv2[rows_of(me, pitch_w, part), :] = snd2[rows_of(me, pitch_w, part), :]
        send(3, half, "dp", in_plane, lambda peer: snd2.at[rows_of(peer, pitch_w, part), :], rcv2.at[rows_of(me, pitch_w, part), :])

    def orthonormalize():
        step = inverse_cholesky(exact_dot(nearly[...], nearly[...], NT))
        nearly[...] = exact_dot(step, nearly[...])
        return step

    @pl.when(me >= 0)
    def _():
        once = orthonormalize()
        whole[...] = exact_dot(orthonormalize(), once)

    for half, part in enumerate(parts_w):
        wait(recv_sem.at[3, half], rcv2, in_plane, counted_w[half])
        total = add_blocks(rcv2, n, pitch_w, counted_w[half])
        here = rows_of(me, pitch_w, part)
        wfull[here, :] = total[0 : part[1] - part[0], :]
        send(4, half, "dp", in_plane, lambda peer: wfull.at[here, :], wfull.at[here, :])
    token_count = total[part[1] - part[0] :, :]

    @pl.when(me >= 0)
    def _():
        upper = exact_dot(orthonormalize(), whole[...]) / token_count[:, 0:1]
        whole_ref[...] = upper
        h, m, l = split3(exact_dot(upper, nearly[...], TN))
        basis_ref[...] = jnp.concatenate((h, h, m, h, l, m), axis=0).T
        scale_ref[...] = jnp.broadcast_to(float(n) / token_count, scale_ref.shape)

    for half, part in enumerate(parts_w):
        wait(recv_sem.at[4, half], wfull, in_plane, part)
        w = collect(wfull, n, pitch_w, part)
        w_ref[:, lanes(part)] = w
        h, m, l = split3(w)
        wcat_ref[:, lanes(part)] = jnp.concatenate((h, m, h, l, h, m), axis=0)

    for phase, peers, parts in ((0, in_plane, parts_p), (1, in_line, parts_p), (2, in_plane, parts_p), (3, in_plane, counted_w), (4, in_plane, parts_w)):
        for half, part in enumerate(parts):
            wait(send_sem.at[phase, half], rcv1, peers, part)


def error_kernel(tile, grad_ref, basis_ref, wcat_ref, w_ref, whole_ref, scale_ref, out_hbm, qt_hbm, out, qt, sem):
    @pl.loop(0, out.shape[0] // tile)
    def _(i):
        here = pl.ds(pl.multiple_of(i * tile, tile), tile)
        approx = jnp.dot(basis_ref[here, :], wcat_ref[...], preferred_element_type=F32)
        out[here, :] = (grad_ref[here, :] * scale_ref[0:1, 0:1] - approx).astype(BF16)
        pltpu.make_async_copy(out.at[here, :], out_hbm.at[here, :], sem.at[0]).start()

    qt[...] = exact_dot(whole_ref[...], w_ref[...])
    qt_copy = pltpu.make_async_copy(qt, qt_hbm, sem.at[1])
    qt_copy.start()
    pltpu.make_async_copy(out, out_hbm, sem.at[0]).wait()
    qt_copy.wait()


def halves(rows, first):
    return [(0, first), (first, rows)]


def largest_tile(length, limit):
    return max(tile for tile in range(LANES, limit + 1, LANES) if length % tile == 0)


def shards(inputs, cotangent, seed_values, counts):
    n, nz = lax.axis_size("dp"), lax.axis_size("tensor")
    tokens, d = inputs.shape
    f = cotangent.shape[1]
    rank = seed_values.shape[1]
    rows_p, rows_w = d // LANES, f // LANES
    pitch_p, pitch_w = round_up(rows_p, 8), round_up(rows_w + 1, 8)
    parts_p, parts_w = halves(rows_p, max(1, rows_p * 2 // 5)), [(0, rows_w)]
    smem, hbm, vmem = (pl.BlockSpec(memory_space=space) for space in (pltpu.SMEM, pltpu.HBM, pltpu.VMEM))
    held = [pltpu.with_memory_space_constraint(array, pltpu.HBM) for array in (inputs, cotangent, seed_values.T)]
    parts = pl.pallas_call(
        functools.partial(exchange_kernel, n, nz, parts_p, parts_w, pitch_p, pitch_w, largest_tile(d, 256)),
        out_shape=(
            pltpu.VMEM((d, f), F32),
            pltpu.VMEM((d, 6 * rank), BF16),
            pltpu.VMEM((6 * rank, f), BF16),
            pltpu.VMEM((rank, f), F32),
            pltpu.VMEM((rank, rank), F32),
            pltpu.VMEM((8, LANES), F32),
        ),
        in_specs=[smem, hbm, hbm, hbm],
        out_specs=(vmem,) * 6,
        scratch_shapes=[
            pltpu.VMEM((tokens, d), BF16),
            pltpu.VMEM((tokens, f), BF16),
            pltpu.VMEM((rank, f), jnp.int32),
            pltpu.VMEM((tokens, f), BF16),
            *[pltpu.VMEM(((n + 1) * round_up(part[1] - part[0], 8), LANES), F32) for part in parts_p],
            pltpu.VMEM((n * pitch_p, LANES), F32),
            pltpu.VMEM((pitch_p, LANES), F32),
            pltpu.VMEM((nz * pitch_p, LANES), F32),
            *[pltpu.VMEM(((n + 1) * round_up(part[1] - part[0], 8), LANES), F32) for part in parts_p],
            pltpu.VMEM(((n + 1) * pitch_w, LANES), F32),
            pltpu.VMEM(((n + 1) * pitch_w, LANES), F32),
            pltpu.VMEM(((n + 1) * pitch_w, LANES), F32),
            pltpu.VMEM((rank, d), F32),
            pltpu.VMEM((rank, rank), F32),
            pltpu.SemaphoreType.DMA((4,)),
            pltpu.SemaphoreType.DMA((5, 2)),
            pltpu.SemaphoreType.DMA((5, 2)),
        ],
        compiler_params=pltpu.CompilerParams(collective_id=0, has_side_effects=True, vmem_limit_bytes=20 << 20),
        name="exchange",
    )(counts, *held)

    new_error, qt = pl.pallas_call(
        functools.partial(error_kernel, largest_tile(d, 640)),
        out_shape=(jax.ShapeDtypeStruct((d, f), BF16), jax.ShapeDtypeStruct((rank, f), F32)),
        in_specs=[vmem] * 6,
        out_specs=(hbm, hbm),
        scratch_shapes=[pltpu.VMEM((d, f), BF16), pltpu.VMEM((rank, f), F32), pltpu.SemaphoreType.DMA((2,))],
        compiler_params=pltpu.CompilerParams(vmem_limit_bytes=18 << 20),
        name="error",
    )(*parts)
    return (new_error[None], qt.T)


def solution(mesh):
    return jax.shard_map(
        shards,
        mesh=mesh,
        in_specs=(P("dp", None), P("dp", "tensor"), P("tensor", None), P("dp")),
        out_specs=(P("dp", None, "tensor"), P("tensor", None)),
        check_vma=False,
    )
```

```python
import functools
import math

import jax
import jax.numpy as jnp
from jax import lax
from jax.experimental import pallas as pl
from jax.experimental.pallas import tpu as pltpu
from jax.sharding import PartitionSpec as P

F32, BF16 = jnp.float32, jnp.bfloat16
LANES = 128
NT = (((1,), (1,)), ((), ()))
TN = (((0,), (0,)), ((), ()))


def round_up(value, unit):
    return -(-value // unit) * unit


def split3(value):
    high = value.astype(BF16)
    rest = value - high.astype(F32)
    mid = rest.astype(BF16)
    low = (rest - mid.astype(F32)).astype(BF16)
    return high, mid, low


def fold3(stacked):
    rows = stacked.shape[0] // 3
    return stacked[:rows] + stacked[rows : 2 * rows] + stacked[2 * rows :]


def exact_dot(left, right, dims=(((1,), (0,)), ((), ()))):
    return lax.dot_general(left, right, dims, precision=lax.Precision.HIGHEST, preferred_element_type=F32)


def inverse_cholesky(gram, group=8):
    size = gram.shape[0]
    row = lax.broadcasted_iota(jnp.int32, (size, size), 0)
    col = lax.broadcasted_iota(jnp.int32, (size, size), 1)
    below = lax.broadcasted_iota(jnp.int32, (size, 1), 0)
    diagonal = jnp.sum(jnp.where(row == col, gram, 0.0), axis=1, keepdims=True)
    floors = jnp.broadcast_to(1e-6 * diagonal, (size, size))
    left, right, scale = gram, (row == col).astype(F32), jnp.ones((size, size), F32)
    for start in range(0, size, group):
        columns = [jnp.broadcast_to(left[:, start + j : start + j + 1], (size, size)) for j in range(group)]
        for j in range(group):
            k = start + j
            pivot = jnp.maximum(columns[j][k : k + 1, :], floors[k : k + 1, :])
            factor = jnp.where(below > k, columns[j] / pivot, 0.0)
            scale = jnp.where(below == k, pivot, scale)
            for i in range(j + 1, group):
                columns[i] = columns[i] - factor * columns[i][k : k + 1, :]
            left, right = left - factor * left[k : k + 1, :], right - factor * right[k : k + 1, :]
    guess = lax.rsqrt(scale)
    return right * (guess * (1.5 - 0.5 * scale * guess * guess))


def spread(ref, value, pitch, first):
    rows, width = value.shape
    for j in range(width // LANES):
        ref[pl.ds(first + j, rows, stride=pitch), :] = value[:, j * LANES : (j + 1) * LANES]


def collect(ref, rows, pitch, part):
    return jnp.concatenate([ref[pl.ds(j, rows, stride=pitch), :] for j in range(*part)], axis=1)


def add_blocks(ref, blocks, pitch, part):
    total = ref[part[0] : part[1], :]
    for i in range(1, blocks):
        total = total + ref[i * pitch + part[0] : i * pitch + part[1], :]
    return total


def lanes(part):
    return pl.ds(part[0] * LANES, (part[1] - part[0]) * LANES)


def ring_distance(step, size):
    return min(step, size - step)


def plane_peers(me, n):
    side = math.isqrt(n // 2)
    y, x, core = me // (2 * side), me // 2 % side, me % 2
    steps = [(dy, dx, dc) for dy in range(side) for dx in range(side) for dc in range(2) if dy or dx or dc]
    far = [-ring_distance(step, side) for step in range(side)]
    steps.sort(key=lambda step: (far[step[0]] + far[step[1]], step[2], (3 * step[0] + 5 * step[1]) % side))
    return [((y + dy) % side * side + (x + dx) % side) * 2 + (core + dc) % 2 for dy, dx, dc in steps]


def line_peers(me, n):
    return [(me + step) % n for step in sorted(range(1, n), key=lambda step: -ring_distance(step, n))]


def exchange_kernel(
    n, nz, parts_p, parts_w, pitch_p, pitch_w, tile,
    count_ref, x_hbm, c_hbm, s_hbm,
    grad_ref, basis_ref, wcat_ref, w_ref, whole_ref, scale_ref,
    x, c, s, live_c, snd1a, snd1b, rcv1, zsnd, zrcv, pfulla, pfullb, snd2, rcv2, wfull, nearly, whole,
    load_sem, send_sem, recv_sem,
):
    me, mz = lax.axis_index("dp"), lax.axis_index("tensor")
    snd1, pfull = (snd1a, snd1b), (pfulla, pfullb)
    tokens, d = x.shape
    in_plane, in_line = plane_peers(me, n), line_peers(mz, nz)

    barrier = pltpu.get_barrier_semaphore()
    for axis, peers in (("dp", in_plane), ("tensor", in_line)):
        for peer in peers:
            pl.semaphore_signal(barrier, inc=1, device_id={axis: peer}, device_id_type=pl.DeviceIdType.MESH)

    pairs = [(s_hbm, s), (c_hbm, c)] + [(x_hbm.at[:, lanes(part)], x.at[:, lanes(part)]) for part in parts_p]
    loads = [pltpu.make_async_copy(src, dst, load_sem.at[i]) for i, (src, dst) in enumerate(pairs)]
    for load in loads:
        load.start()

    def rows_of(index, pitch, part):
        return pl.ds(index * pitch + part[0], part[1] - part[0])

    def send(phase, half, axis, peers, source, target):
        for peer in peers:
            pltpu.make_async_remote_copy(
                src_ref=source(peer), dst_ref=target, send_sem=send_sem.at[phase, half], recv_sem=recv_sem.at[phase, half],
                device_id={axis: peer}, device_id_type=pl.DeviceIdType.MESH,
            ).start()

    def wait(sem, ref, peers, part):
        here = ref.at[pl.ds(0, len(peers) * (part[1] - part[0])), :]
        pltpu.make_async_copy(here, here, sem).wait()

    def weight_grad(first, last):
        @pl.loop(first, last)
        def _(i):
            here = pl.ds(pl.multiple_of(i * tile, tile), tile)
            grad_ref[here, :] = lax.dot_general(x[:, here], live_c[...], TN, preferred_element_type=F32)

    live = lax.broadcasted_iota(jnp.int32, (n, tokens), 1) < count_ref[0]
    tiles = d // tile
    pitches_p = [round_up(part[1] - part[0], 8) for part in parts_p]
    counted_w = parts_w[:-1] + [(parts_w[-1][0], parts_w[-1][1] + 1)]

    loads[0].wait()
    loads[1].wait()
    narrow = lax.dot_general((s[...].astype(F32) / 64.0).astype(BF16), c[...], NT, preferred_element_type=F32)
    narrow = jnp.concatenate(split3(jnp.where(live, narrow, 0.0)), axis=0)
    for half, part in enumerate(parts_p):
        loads[2 + half].wait()
        spread(snd1[half], fold3(jnp.dot(narrow, x[:, lanes(part)], preferred_element_type=F32)), pitches_p[half], 0)
        if half == 0:
            pl.semaphore_wait(barrier, n - 1 + nz - 1)
        send(0, half, "dp", in_plane, lambda peer: snd1[half].at[pl.ds(peer * pitches_p[half], part[1] - part[0]), :], rcv1.at[rows_of(me, pitch_p, part), :])
    for half, part in enumerate(parts_p):
        rcv1[rows_of(me, pitch_p, part), :] = snd1[half][pl.ds(me * pitches_p[half], part[1] - part[0]), :]
    position = lax.broadcasted_iota(jnp.int32, live_c.shape, 0)
    live_c[...] = jnp.where(position < count_ref[0], c[...], jnp.zeros_like(c))
    weight_grad(0, tiles // 2)

    for half, part in enumerate(parts_p):
        wait(recv_sem.at[0, half], rcv1, in_plane, part)
        mine = add_blocks(rcv1, n, pitch_p, part)
        zsnd[rows_of(0, pitch_p, part), :] = mine
        send(1, half, "tensor", in_line, lambda peer: zsnd.at[rows_of(0, pitch_p, part), :], zrcv.at[rows_of(mz, pitch_p, part), :])
        zrcv[rows_of(mz, pitch_p, part), :] = mine
    weight_grad(tiles // 2, tiles)

    for half, part in enumerate(parts_p):
        wait(recv_sem.at[1, half], zrcv, in_line, part)
        mine = pfull[half].at[pl.ds(me * pitches_p[half], part[1] - part[0]), :]
        mine[...] = add_blocks(zrcv, nz, pitch_p, part)
        send(2, half, "dp", in_plane, lambda peer: mine, mine)

    projected = 0.0
    for half, part in enumerate(parts_p):
        wait(recv_sem.at[2, half], pfull[half], in_plane, part)
        left = collect(pfull[half], n, pitches_p[half], (0, part[1] - part[0]))
        nearly[:, lanes(part)] = left
        projected = projected + lax.dot_general(
            jnp.concatenate(split3(left), axis=0), x[:, lanes(part)], NT, preferred_element_type=F32
        )
    projected = jnp.concatenate(split3(jnp.where(live, fold3(projected), 0.0)), axis=0)
    snd2[pl.ds(parts_w[-1][1], n, stride=pitch_w), :] = jnp.full((n, LANES), count_ref[0], jnp.int32).astype(F32)
    spread(snd2, fold3(jnp.dot(projected, c[...], preferred_element_type=F32)), pitch_w, 0)
    for half, part in enumerate(counted_w):
        send(3, half, "dp", in_plane, lambda peer: snd2.at[rows_of(peer, pitch_w, part), :], rcv2.at[rows_of(me, pitch_w, part), :])
        rcv2[rows_of(me, pitch_w, part), :] = snd2[rows_of(me, pitch_w, part), :]

    def orthonormalize():
        step = inverse_cholesky(exact_dot(nearly[...], nearly[...], NT))
        nearly[...] = exact_dot(step, nearly[...])
        return step

    @pl.when(me >= 0)
    def _():
        once = orthonormalize()
        whole[...] = exact_dot(orthonormalize(), once)

    for half, part in enumerate(parts_w):
        wait(recv_sem.at[3, half], rcv2, in_plane, counted_w[half])
        total = add_blocks(rcv2, n, pitch_w, counted_w[half])
        here = rows_of(me, pitch_w, part)
        wfull[here, :] = total[0 : part[1] - part[0], :]
        send(4, half, "dp", in_plane, lambda peer: wfull.at[here, :], wfull.at[here, :])
    token_count = total[part[1] - part[0] :, :]

    @pl.when(me >= 0)
    def _():
        upper = exact_dot(orthonormalize(), whole[...]) / token_count[:, 0:1]
        whole_ref[...] = upper
        h, m, l = split3(exact_dot(upper, nearly[...], TN))
        basis_ref[...] = jnp.concatenate((h, h, m, h, l, m), axis=0).T
        scale_ref[...] = jnp.broadcast_to(float(n) / token_count, scale_ref.shape)

    for half, part in enumerate(parts_w):
        wait(recv_sem.at[4, half], wfull, in_plane, part)
        w = collect(wfull, n, pitch_w, part)
        w_ref[:, lanes(part)] = w
        h, m, l = split3(w)
        wcat_ref[:, lanes(part)] = jnp.concatenate((h, m, h, l, h, m), axis=0)

    for phase, peers, parts in ((0, in_plane, parts_p), (1, in_line, parts_p), (2, in_plane, parts_p), (3, in_plane, counted_w), (4, in_plane, parts_w)):
        for half, part in enumerate(parts):
            wait(send_sem.at[phase, half], rcv1, peers, part)


def error_kernel(tile, grad_ref, basis_ref, wcat_ref, w_ref, whole_ref, scale_ref, out_hbm, qt_hbm, out, qt, sem):
    @pl.loop(0, out.shape[0] // tile)
    def _(i):
        here = pl.ds(pl.multiple_of(i * tile, tile), tile)
        approx = jnp.dot(basis_ref[here, :], wcat_ref[...], preferred_element_type=F32)
        out[here, :] = (grad_ref[here, :] * scale_ref[0:1, 0:1] - approx).astype(BF16)
        pltpu.make_async_copy(out.at[here, :], out_hbm.at[here, :], sem.at[0]).start()

    qt[...] = exact_dot(whole_ref[...], w_ref[...])
    qt_copy = pltpu.make_async_copy(qt, qt_hbm, sem.at[1])
    qt_copy.start()
    pltpu.make_async_copy(out, out_hbm, sem.at[0]).wait()
    qt_copy.wait()


def halves(rows, first):
    return [(0, first), (first, rows)]


def largest_tile(length, limit):
    return max(tile for tile in range(LANES, limit + 1, LANES) if length % tile == 0)


def shards(inputs, cotangent, seed_values, counts):
    n, nz = lax.axis_size("dp"), lax.axis_size("tensor")
    tokens, d = inputs.shape
    f = cotangent.shape[1]
    rank = seed_values.shape[1]
    rows_p, rows_w = d // LANES, f // LANES
    pitch_p, pitch_w = round_up(rows_p, 8), round_up(rows_w + 1, 8)
    parts_p, parts_w = halves(rows_p, max(1, rows_p * 2 // 5)), [(0, rows_w)]
    smem, hbm, vmem = (pl.BlockSpec(memory_space=space) for space in (pltpu.SMEM, pltpu.HBM, pltpu.VMEM))
    held = [pltpu.with_memory_space_constraint(array, pltpu.HBM) for array in (inputs, cotangent, seed_values.T)]
    parts = pl.pallas_call(
        functools.partial(exchange_kernel, n, nz, parts_p, parts_w, pitch_p, pitch_w, largest_tile(d, 256)),
        out_shape=(
            pltpu.VMEM((d, f), F32),
            pltpu.VMEM((d, 6 * rank), BF16),
            pltpu.VMEM((6 * rank, f), BF16),
            pltpu.VMEM((rank, f), F32),
            pltpu.VMEM((rank, rank), F32),
            pltpu.VMEM((8, LANES), F32),
        ),
        in_specs=[smem, hbm, hbm, hbm],
        out_specs=(vmem,) * 6,
        scratch_shapes=[
            pltpu.VMEM((tokens, d), BF16),
            pltpu.VMEM((tokens, f), BF16),
            pltpu.VMEM((rank, f), jnp.int32),
            pltpu.VMEM((tokens, f), BF16),
            *[pltpu.VMEM(((n + 1) * round_up(part[1] - part[0], 8), LANES), F32) for part in parts_p],
            pltpu.VMEM((n * pitch_p, LANES), F32),
            pltpu.VMEM((pitch_p, LANES), F32),
            pltpu.VMEM((nz * pitch_p, LANES), F32),
            *[pltpu.VMEM(((n + 1) * round_up(part[1] - part[0], 8), LANES), F32) for part in parts_p],
            pltpu.VMEM(((n + 1) * pitch_w, LANES), F32),
            pltpu.VMEM(((n + 1) * pitch_w, LANES), F32),
            pltpu.VMEM(((n + 1) * pitch_w, LANES), F32),
            pltpu.VMEM((rank, d), F32),
            pltpu.VMEM((rank, rank), F32),
            pltpu.SemaphoreType.DMA((4,)),
            pltpu.SemaphoreType.DMA((5, 2)),
            pltpu.SemaphoreType.DMA((5, 2)),
        ],
        compiler_params=pltpu.CompilerParams(collective_id=0, has_side_effects=True, vmem_limit_bytes=20 << 20),
        name="exchange",
    )(counts, *held)

    new_error, qt = pl.pallas_call(
        functools.partial(error_kernel, largest_tile(d, 640)),
        out_shape=(jax.ShapeDtypeStruct((d, f), BF16), jax.ShapeDtypeStruct((rank, f), F32)),
        in_specs=[vmem] * 6,
        out_specs=(hbm, hbm),
        scratch_shapes=[pltpu.VMEM((d, f), BF16), pltpu.VMEM((rank, f), F32), pltpu.SemaphoreType.DMA((2,))],
        compiler_params=pltpu.CompilerParams(vmem_limit_bytes=18 << 20),
        name="error",
    )(*parts)
    return (new_error[None], qt.T)


def solution(mesh):
    return jax.shard_map(
        shards,
        mesh=mesh,
        in_specs=(P("dp", None), P("dp", "tensor"), P("tensor", None), P("dp")),
        out_specs=(P("dp", None, "tensor"), P("tensor", None)),
        check_vma=False,
    )
```
